32 devices in a mesh: groups: 2 (over x), tensor: 16 (over z, y, core).
Axes of the slice: x: 2, y: 2, z: 4, core: 2. Of those that a mesh axis runs over, the one named last changes fastest.
Arguments:
- tokens: bfloat16 [256, 8192], P(('groups', 'tensor')), parts along dimension 0, may hold values from -6 to 6
- gate_weight: bfloat16 [8192, 28672], P(None, 'tensor'), may hold values from -0.0625 to 0.0625
- up_weight: bfloat16 [8192, 28672], P(None, 'tensor'), may hold values from -0.0625 to 0.0625
- first_store: bfloat16 [64, 16, 32, 512], P(('groups', 'tensor')), parts along dimension 0, may hold values from -0.0625 to 0.0625
- second_store: bfloat16 [64, 16, 32, 1792], P(('groups', 'tensor')), parts along dimension 0, may hold values from -1.5 to 1.5
- adapter_ids: int32 [2], P('groups'), parts along dimension 0, may hold values from 0 to 31
- owner_map: int32 [64], P('groups'), parts along dimension 0, may hold values from 0 to 31, each once
Outputs:
- hidden: bfloat16 [256, 28672], P('groups', 'tensor'), parts along dimension 0
The draws below stay inside these ranges and needn't reach their ends.
There are 2 independent parts, one for each index of `groups`. The reference program is written for one: setup_inputs(seed, part) draws one part's arguments, and reference() takes and returns one part's arrays. A program takes and returns all parts, laid end to end along the dimension named above; an argument that names none is the same for every part. Nothing has to cross between parts.
Inputs may be any that keep to these rules, and one draw needn't show every extreme that they name: `adapter_ids`: prompt p covers tokens p * 128 to (p + 1) * 128 - 1. `owner_map`: A permutation of the slots: slot s is entry s % 2 of the store of index s // 2 of tensor.
All inputs are finite; a program needn't handle non-finite values.
Results may differ from the reference program's by a relative error of at most 0.0051.
Values may be sent and summed in bfloat16 or wider, within the bound.
A program may use at most 192 MiB of HBM per device.

```python
import math
import jax
import jax.numpy as jnp
import numpy as np
from jax import lax

D = 8192
FF = 28672
RANK = 16
PLEN = 128
TOKENS = 128
PROMPTS = 1
ADAPTERS = 32
N_TENSOR = 16


def block_scale(rng, dims, split, least, top_value):
    def one(axis_at, blocks):
        steps = jax.random.uniform(jax.random.fold_in(jax.random.fold_in(rng, 6), axis_at), (blocks,), jnp.float32, least / len(split), top_value / len(split))
        return jnp.repeat(jnp.exp(steps), dims[axis_at] // blocks).reshape((-1,) + (1,) * (len(dims) - axis_at - 1))

    gain = one(*split[0])
    for cut in split[1:]:
        gain = gain * one(*cut)
    return gain


def cumulative_ranks(count, skew):
    portions = [(1 << 20) // math.isqrt(grade ** skew) + 1 for grade in range(1, count + 1)]
    deviation = 1 + sum(portions) // (1 << 30)
    return np.cumsum(np.array([max(1, weight // deviation) for weight in portions]))


def ranked_ids(stream_key, dims, count, skew):
    table = cumulative_ranks(count, skew)
    lot = jax.random.randint(jax.random.fold_in(stream_key, 1), dims, 0, int(table[count - 1]))
    grade = jnp.searchsorted(jnp.asarray(table, jnp.int32), lot, side="right")
    return jax.random.permutation(jax.random.fold_in(stream_key, 2), count)[grade].astype(jnp.int32)


def bell_draw(rng, extent, scale, reach, pieces=(), dtype=jnp.bfloat16):
    result = scale * jax.random.normal(rng, extent, jnp.float32)
    if pieces:
        result = result * block_scale(rng, extent, pieces, -0.22, 0.18)
    return jnp.clip(result, -reach, reach).astype(dtype)


def setup_inputs(seed: int = 0, part: int = 0) -> dict:
    streams_of = jax.random.split(jax.random.key(seed), 8)
    part_keys = jax.random.split(jax.random.fold_in(streams_of[7], part), 8)
    tokens = bell_draw(part_keys[0], (TOKENS, D), 1.0, 6.0, ((0, 16),))
    gate_weight = bell_draw(streams_of[1], (D, FF), D ** -0.5, 0.0625, ((1, 16),))
    up_weight = bell_draw(streams_of[2], (D, FF), D ** -0.5, 0.0625, ((1, 16),))
    first_store = bell_draw(part_keys[3], (ADAPTERS, N_TENSOR, 2 * RANK, D // N_TENSOR), D ** -0.5, 0.0625, ((0, 16),))
    second_store = bell_draw(part_keys[4], (ADAPTERS, N_TENSOR, 2 * RANK, FF // N_TENSOR), RANK ** -0.5, 1.5, ((0, 16),))
    adapter_ids = ranked_ids(part_keys[5], (PROMPTS,), ADAPTERS, 2)
    owner_map = jax.random.permutation(part_keys[6], ADAPTERS).astype(jnp.int32)
    return dict(tokens=tokens, gate_weight=gate_weight, up_weight=up_weight, first_store=first_store, second_store=second_store, adapter_ids=adapter_ids, owner_map=owner_map)


def reference(tokens, gate_weight, up_weight, first_store, second_store, adapter_ids, owner_map):
    prompts = adapter_ids.shape[0]
    slots = owner_map[adapter_ids]
    picked_first = first_store[slots].astype(jnp.float32)
    picked_first = jnp.transpose(picked_first, (0, 2, 1, 3)).reshape(prompts, 2 * RANK, D)
    rows3 = tokens.reshape(prompts, PLEN, D).astype(jnp.float32)
    lowrank = jnp.einsum('ptd,pkd->ptk', rows3, picked_first).astype(jnp.bfloat16)
    lowrank = lax.optimization_barrier(lowrank)
    low_four = lowrank.astype(jnp.float32).reshape(prompts, PLEN, 2, RANK)
    picked_second = second_store[slots].astype(jnp.float32)
    picked_second = jnp.transpose(picked_second, (0, 2, 1, 3)).reshape(prompts, 2, RANK, FF)
    delta = jnp.einsum('ptgr,pgrf->gptf', low_four, picked_second).reshape(2, prompts * PLEN, FF)
    gate = jnp.dot(tokens, gate_weight, preferred_element_type=jnp.float32) + delta[0]
    lifted = jnp.dot(tokens, up_weight, preferred_element_type=jnp.float32) + delta[1]
    return (jax.nn.silu(gate) * lifted).astype(jnp.bfloat16)
```

```python
import functools
import jax
import jax.numpy as jnp
from jax import lax
from jax.experimental import pallas as pl
from jax.experimental.pallas import tpu as pltpu
from jax.sharding import PartitionSpec as P

PLEN = 128
CHUNKS = 8
SLOTS = 12
R1_AT, R2_AT = 4, 9
MESH = pl.DeviceIdType.MESH


def spread(value, axis, root):
    mine = lax.axis_index(axis) == root
    return lax.psum(jnp.where(mine, value, jnp.zeros_like(value)), axis)


def general(tokens, gate_weight, up_weight, first_store, second_store, adapter_ids, owner_map):
    own_index = lax.axis_index("tensor")
    tok_dev = tokens.shape[0]
    prompts = adapter_ids.shape[0]
    keep_count = first_store.shape[0]
    doubled = second_store.shape[2]
    rank = doubled // 2
    width = gate_weight.shape[1]
    matches = adapter_ids[:, None] == jnp.arange(owner_map.shape[0], dtype=jnp.int32)[None, :]
    slots = jnp.sum(jnp.where(matches, owner_map[None, :], 0), axis=1)
    own_prompt = own_index * tok_dev // PLEN

    def fetch_step(prompt, held):
        slot = lax.dynamic_index_in_dim(slots, prompt, 0, keepdims=False)
        piece = lax.dynamic_index_in_dim(first_store, slot % keep_count, 0, keepdims=False)
        landed = spread(piece, "tensor", slot // keep_count)
        return jnp.where(prompt == own_prompt, landed, held)

    blocked = lax.fori_loop(0, prompts, fetch_step, jnp.zeros(first_store.shape[1:], jnp.bfloat16))
    factor = jnp.transpose(blocked, (1, 0, 2)).reshape(doubled, tokens.shape[1])
    lowrank = jnp.dot(tokens, factor.T, preferred_element_type=jnp.float32).astype(jnp.bfloat16)
    whole, low_all = (
        lax.all_gather(tokens, "tensor", axis=0, tiled=True),
        lax.all_gather(lowrank, "tensor", axis=0, tiled=True),
    )
    spread_second = lax.all_to_all(second_store, "tensor", split_axis=1, concat_axis=0, tiled=True)
    spread_second = spread_second.reshape(spread_second.shape[0], 2, rank, width)
    picked_second = jnp.take(spread_second, slots, axis=0)
    low_four = low_all.reshape(prompts, PLEN, 2, rank)
    delta = jnp.einsum(
        "ptgr,pgrf->gptf", low_four, picked_second, preferred_element_type=jnp.float32
    )
    delta = delta.reshape(2, prompts * PLEN, width)
    gate = jnp.dot(whole, gate_weight, preferred_element_type=jnp.float32) + delta[0]
    lifted = jnp.dot(whole, up_weight, preferred_element_type=jnp.float32) + delta[1]
    return (jax.nn.silu(gate) * lifted).astype(jnp.bfloat16)


def kernel(
    nz, keep,
    tok, wg, wu, f1, ss, ids, omap, out,
    x, xf, w, ag, au, pbuf, sbuf, qbuf, tbuf, fbuf, lacc, lstage, lc, ly, lz,
    s_tok, s_w, s_p, zs, zr, ys, yr, cs, cr, ps, pr, rys, ryr, rzs, rzr, ls, lr,
):
    me = lax.axis_index("tensor")
    core = lax.rem(me, 2)
    yy = lax.rem(me // 2, 2)
    zz = me // 4
    kc = xf.shape[2]
    width = wg.shape[1]
    sub = kc // f1.shape[3]
    nw = 2 * CHUNKS

    def at(z, y, c):
        return {"tensor": z * 4 + y * 2 + c}

    def far(d):
        return lax.rem(zz + d, nz)

    def near(d):
        return lax.rem(zz + nz - d, nz)

    def remote(src, dst, send, recv, dev):
        return pltpu.make_async_remote_copy(
            src_ref=src, dst_ref=dst, send_sem=send, recv_sem=recv,
            device_id=dev, device_id_type=MESH,
        )

    def w_copy(src, chunk, half):
        slot = lax.rem(chunk * 2 + half, SLOTS)
        rows = pl.ds(pl.multiple_of(chunk * kc, kc), kc)
        return pltpu.make_async_copy(src.at[rows, :], w.at[slot], s_w.at[slot])

    partners = [at(zz, yy, 1 - core), at(zz, 1 - yy, core)]
    partners += [at(far(d), yy, core) for d in range(1, nz)]
    barrier = pltpu.get_barrier_semaphore()
    for dev in partners:
        pl.semaphore_signal(barrier, inc=1, device_id=dev, device_id_type=MESH)

    def cols(ch):
        return pl.ds(pl.multiple_of(ch * kc, kc), kc)

    def own_copy(ch):
        return pltpu.make_async_copy(
            tok.at[:, cols(ch)], x.at[ch, core, yy, zz], s_tok.at[ch]
        )

    def z_copy(ch, d):
        return remote(
            tok.at[:, cols(ch)], x.at[ch, core, yy, zz],
            zs.at[ch, d - 1], zr.at[ch, d - 1], at(far(d), yy, core),
        )

    def z_wait(ch, d):
        remote(
            tok.at[:, cols(ch)], x.at[ch, core, yy, near(d)],
            zs.at[ch, d - 1], zr.at[ch, d - 1], at(far(d), yy, core),
        ).wait_recv()

    def y_copy(ch, side):
        part = x.at[ch, core, side]
        return remote(part, part, ys.at[ch], yr.at[ch], at(zz, 1 - yy, core))

    def c_copy(ch, side):
        part = x.at[ch, side]
        return remote(part, part, cs.at[ch], cr.at[ch], at(zz, yy, 1 - core))

    own_p = pltpu.make_async_copy(ss.at[:, :, :, core], pbuf.at[pl.ds(0, keep)], s_p.at[0])
    far_p = remote(
        ss.at[:, :, :, 1 - core], pbuf.at[pl.ds(keep, keep)], ps.at[0], pr.at[0],
        at(zz, yy, 1 - core),
    )

    def ry_copy(z):
        return remote(
            sbuf.at[z], qbuf.at[yy, z], rys.at[z], ryr.at[z], at(zz, 1 - yy, core)
        )

    def rz_copy(d):
        return remote(
            tbuf.at[far(d)], fbuf.at[zz], rzs.at[d - 1], rzr.at[d - 1], at(far(d), yy, core)
        )

    def l_copy(hop, src, dst, dev):
        return remote(src, dst, ls.at[hop], lr.at[hop], dev)

    l_core = l_copy(0, lc.at[core], lc.at[core], at(zz, yy, 1 - core))
    l_y = l_copy(1, ly.at[yy], ly.at[yy], at(zz, 1 - yy, core))

    def l_z(d):
        return l_copy(1 + d, lz.at[zz], lz.at[zz], at(far(d), yy, core))

    def own_loop(ch, _):
        own_copy(ch).start()
        return 0

    lax.fori_loop(0, CHUNKS, own_loop, 0)
    for j in range(SLOTS // 2):
        w_copy(wg, j, 0).start()
        w_copy(wu, j, 1).start()
    own_p.start()
    slot = omap[ids[0]]
    kslot = lax.rem(slot, keep)
    owner = slot // keep
    oc = lax.rem(owner, 2)
    oy = lax.rem(owner // 2, 2)
    oz = owner // 4
    pick = jnp.where(oc == core, 0, keep) + kslot
    ag[...] = jnp.zeros_like(ag)
    au[...] = jnp.zeros_like(au)
    lacc[...] = jnp.zeros_like(lacc)
    pl.semaphore_wait(barrier, len(partners))

    def z_loop(ch, _):
        for d in range(1, nz):
            z_copy(ch, d).start()
        return 0

    lax.fori_loop(0, CHUNKS, z_loop, 0)
    far_p.start()

    def step(i, _):
        @pl.when(i < CHUNKS)
        def _():
            own_copy(i).wait()
            for d in range(1, nz):
                z_wait(i, d)
            y_copy(i, yy).start()

        @pl.when((i >= 1) & (i < CHUNKS + 1))
        def _():
            ch = i - 1
            y_copy(ch, 1 - yy).wait_recv()
            c_copy(ch, core).start()

        @pl.when((i >= 2) & (i < CHUNKS + 2))
        def _():
            ch = i - 2
            c_copy(ch, 1 - core).wait_recv()
            for z in range(nz):
                for y in range(2):
                    a = x[ch, 0, y, z].astype(jnp.float32)
                    b = x[ch, 1, y, z].astype(jnp.float32)
                    m = 16 * (z * 2 + y)
                    xf[ch, m:m + 16, :] = jnp.concatenate([a, b], 0).astype(jnp.bfloat16)
            size = f1.shape[3]
            for s in range(sub):
                lacc[...] += lax.dot_general(
                    f1[kslot, ch * sub + s], xf[ch, :, s * size:(s + 1) * size],
                    (((1,), (1,)), ((), ())), preferred_element_type=jnp.float32,
                )

        @pl.when(i == R1_AT)
        def _():
            own_p.wait()
            far_p.wait_recv()
            for z in range(nz):
                sbuf[z] = pbuf[pick, z, 1 - yy]
                ry_copy(z).start()
                tbuf[z] = pbuf[pick, z, yy]

        @pl.when(i == R2_AT)
        def _():
            for z in range(nz):
                remote(
                    sbuf.at[z], qbuf.at[1 - yy, z], rys.at[z], ryr.at[z],
                    at(zz, 1 - yy, core),
                ).wait_recv()
                qbuf[yy, z] = tbuf[z]
            for z in range(nz):
                tbuf[z] = qbuf[oy, z]
            for d in range(1, nz):
                rz_copy(d).start()
            fbuf[zz] = tbuf[zz]

        @pl.when(i == CHUNKS + 1)
        def _():
            lc[core] = lacc[...].astype(jnp.bfloat16)
            l_core.start()

        @pl.when(i == CHUNKS + 2)
        def _():
            l_copy(0, lc.at[core], lc.at[1 - core], at(zz, yy, 1 - core)).wait_recv()
            ly[yy] = lc[oc]
            l_y.start()

        @pl.when(i >= 3)
        def _():
            ch = i - 3
            for half, src, acc in ((0, wg, ag), (1, wu, au)):
                w_copy(src, ch, half).wait()
                slot_w = lax.rem(ch * 2 + half, SLOTS)
                for n in range(0, width, 256):
                    acc[:, n:n + 256] += jnp.dot(
                        xf[ch], w[slot_w, :, n:n + 256], preferred_element_type=jnp.float32
                    )

                @pl.when(ch + SLOTS // 2 < CHUNKS)
                def _():
                    w_copy(src, ch + SLOTS // 2, half).start()

        return 0

    lax.fori_loop(0, CHUNKS + 3, step, 0)

    l_copy(1, ly.at[yy], ly.at[1 - yy], at(zz, 1 - yy, core)).wait_recv()
    lz[zz] = ly[oy]
    for d in range(1, nz):
        l_z(d).start()
    for d in range(1, nz):
        remote(
            tbuf.at[far(d)], fbuf.at[near(d)], rzs.at[d - 1], rzr.at[d - 1],
            at(far(d), yy, core),
        ).wait_recv()
    for d in range(1, nz):
        l_copy(1 + d, lz.at[zz], lz.at[near(d)], at(far(d), yy, core)).wait_recv()
    lstage[...] = lz[oz]
    rank = lstage.shape[0] // 2
    dims = (((0,), (0,)), ((), ()))
    for n in range(0, width, 256):
        g = ag[:, n:n + 256] + lax.dot_general(
            lstage[:rank], fbuf[oz, :rank, n:n + 256], dims, preferred_element_type=jnp.float32
        )
        u = au[:, n:n + 256] + lax.dot_general(
            lstage[rank:], fbuf[oz, rank:, n:n + 256], dims, preferred_element_type=jnp.float32
        )
        out[:, n:n + 256] = (g / (1.0 + jnp.exp(-g)) * u).astype(out.dtype)

    def drain(ch, _):
        for d in range(1, nz):
            z_copy(ch, d).wait_send()
        y_copy(ch, yy).wait_send()
        c_copy(ch, core).wait_send()
        return 0

    lax.fori_loop(0, CHUNKS, drain, 0)
    far_p.wait_send()
    for z in range(nz):
        ry_copy(z).wait_send()
    for d in range(1, nz):
        rz_copy(d).wait_send()
        l_z(d).wait_send()
    l_core.wait_send()
    l_y.wait_send()


def fused(tensor, tokens, gate_weight, up_weight, first_store, second_store, adapter_ids, owner_map):
    nz = tensor // 4
    keep = first_store.shape[0]
    doubled, width = second_store.shape[2:]
    depth = tokens.shape[1]
    kc = depth // CHUNKS
    rows = tokens.shape[0] * tensor
    second = second_store.reshape(keep, nz, 2, 2, doubled, width)
    any_, vmem, smem = (
        pl.BlockSpec(memory_space=s) for s in (pl.ANY, pltpu.VMEM, pltpu.SMEM)
    )
    bf, f32 = jnp.bfloat16, jnp.float32
    dma = pltpu.SemaphoreType.DMA
    return pl.pallas_call(
        functools.partial(kernel, nz, keep),
        out_shape=jax.ShapeDtypeStruct((rows, width), bf),
        in_specs=[any_, any_, any_, vmem, any_, smem, smem],
        out_specs=vmem,
        scratch_shapes=[
            pltpu.VMEM((CHUNKS, 2, 2, nz, tokens.shape[0], kc), bf),
            pltpu.VMEM((CHUNKS, rows, kc), bf),
            pltpu.VMEM((SLOTS, kc, width), bf),
            pltpu.VMEM((rows, width), f32),
            pltpu.VMEM((rows, width), f32),
            pltpu.VMEM((2 * keep, nz, 2, doubled, width), bf),
            pltpu.VMEM((nz, doubled, width), bf),
            pltpu.VMEM((2, nz, doubled, width), bf),
            pltpu.VMEM((nz, doubled, width), bf),
            pltpu.VMEM((nz, doubled, width), bf),
            pltpu.VMEM((doubled, rows), f32),
            pltpu.VMEM((doubled, rows), bf),
            pltpu.VMEM((2, doubled, rows), bf),
            pltpu.VMEM((2, doubled, rows), bf),
            pltpu.VMEM((nz, doubled, rows), bf),
            dma((CHUNKS,)), dma((SLOTS,)), dma((1,)),
            dma((CHUNKS, nz - 1)), dma((CHUNKS, nz - 1)),
            dma((CHUNKS,)), dma((CHUNKS,)), dma((CHUNKS,)), dma((CHUNKS,)),
            dma((1,)), dma((1,)), dma((nz,)), dma((nz,)), dma((nz - 1,)), dma((nz - 1,)),
            dma((nz + 1,)), dma((nz + 1,)),
        ],
        compiler_params=pltpu.CompilerParams(
            collective_id=0, has_side_effects=True, vmem_limit_bytes=63 * 1024 * 1024
        ),
        cost_estimate=pl.CostEstimate(
            flops=4 * rows * depth * width, bytes_accessed=4 * depth * width,
            transcendentals=rows * width,
        ),
    )(tokens, gate_weight, up_weight, first_store, second, adapter_ids, owner_map)


def solution(mesh):
    tensor = mesh.shape["tensor"]

    def per_device(*args):
        if tensor == 16 and args[5].shape[0] == 1:
            return fused(tensor, *args)
        return general(*args)

    placed = (
        P(("groups", "tensor"), None),
        P(None, "tensor"),
        P(None, "tensor"),
        P(("groups", "tensor"), None, None, None),
        P(("groups", "tensor"), None, None, None),
        P("groups"),
        P("groups"),
    )
    return jax.shard_map(
        per_device, mesh=mesh, in_specs=placed, out_specs=P("groups", "tensor"), check_vma=False
    )
```

```python
import functools
import jax
import jax.numpy as jnp
from jax import lax
from jax.experimental import pallas as pl
from jax.experimental.pallas import tpu as pltpu
from jax.sharding import PartitionSpec as P

PLEN = 128
CHUNKS = 4
SLOTS = 6
R1_AT, R2_AT = 2, (6, 4, 5, 6)
MESH = pl.DeviceIdType.MESH


def spread(value, axis, root):
    mine = lax.axis_index(axis) == root
    return lax.psum(jnp.where(mine, value, jnp.zeros_like(value)), axis)


def general(tokens, gate_weight, up_weight, first_store, second_store, adapter_ids, owner_map):
    own_index = lax.axis_index("tensor")
    tok_dev = tokens.shape[0]
    prompts = adapter_ids.shape[0]
    keep_count = first_store.shape[0]
    doubled = second_store.shape[2]
    rank = doubled // 2
    width = gate_weight.shape[1]
    matches = adapter_ids[:, None] == jnp.arange(owner_map.shape[0], dtype=jnp.int32)[None, :]
    slots = jnp.sum(jnp.where(matches, owner_map[None, :], 0), axis=1)
    own_prompt = own_index * tok_dev // PLEN

    def fetch_step(prompt, held):
        slot = lax.dynamic_index_in_dim(slots, prompt, 0, keepdims=False)
        piece = lax.dynamic_index_in_dim(first_store, slot % keep_count, 0, keepdims=False)
        landed = spread(piece, "tensor", slot // keep_count)
        return jnp.where(prompt == own_prompt, landed, held)

    blocked = lax.fori_loop(0, prompts, fetch_step, jnp.zeros(first_store.shape[1:], jnp.bfloat16))
    factor = jnp.transpose(blocked, (1, 0, 2)).reshape(doubled, tokens.shape[1])
    lowrank = jnp.dot(tokens, factor.T, preferred_element_type=jnp.float32).astype(jnp.bfloat16)
    whole, low_all = (
        lax.all_gather(tokens, "tensor", axis=0, tiled=True),
        lax.all_gather(lowrank, "tensor", axis=0, tiled=True),
    )
    spread_second = lax.all_to_all(second_store, "tensor", split_axis=1, concat_axis=0, tiled=True)
    spread_second = spread_second.reshape(spread_second.shape[0], 2, rank, width)
    picked_second = jnp.take(spread_second, slots, axis=0)
    low_four = low_all.reshape(prompts, PLEN, 2, rank)
    delta = jnp.einsum(
        "ptgr,pgrf->gptf", low_four, picked_second, preferred_element_type=jnp.float32
    )
    delta = delta.reshape(2, prompts * PLEN, width)
    gate = jnp.dot(whole, gate_weight, preferred_element_type=jnp.float32) + delta[0]
    lifted = jnp.dot(whole, up_weight, preferred_element_type=jnp.float32) + delta[1]
    return (jax.nn.silu(gate) * lifted).astype(jnp.bfloat16)


def kernel(
    nz, keep,
    tok, wg, wu, f1, ss, ids, omap, out,
    x, xf, w, ag, au, pbuf, sbuf, qbuf, tbuf, fbuf, lacc, lstage, lc, ly, lz,
    s_tok, s_w, s_p, zs, zr, ys, yr, cs, cr, ps, pr, rys, ryr, rzs, rzr, ls, lr,
):
    me = lax.axis_index("tensor")
    core = lax.rem(me, 2)
    yy = lax.rem(me // 2, 2)
    zz = me // 4
    kc = xf.shape[2]
    width = wg.shape[1]
    sub = kc // f1.shape[3]
    nw = 2 * CHUNKS

    def at(z, y, c):
        return {"tensor": z * 4 + y * 2 + c}

    def far(d):
        return lax.rem(zz + d, nz)

    def near(d):
        return lax.rem(zz + nz - d, nz)

    def remote(src, dst, send, recv, dev):
        return pltpu.make_async_remote_copy(
            src_ref=src, dst_ref=dst, send_sem=send, recv_sem=recv,
            device_id=dev, device_id_type=MESH,
        )

    def w_copy(src, chunk, half):
        slot = lax.rem(chunk * 2 + half, SLOTS)
        rows = pl.ds(pl.multiple_of(chunk * kc, kc), kc)
        return pltpu.make_async_copy(src.at[rows, :], w.at[slot], s_w.at[slot])

    partners = [at(zz, yy, 1 - core), at(zz, 1 - yy, core)]
    partners += [at(far(d), yy, core) for d in range(1, nz)]
    barrier = pltpu.get_barrier_semaphore()
    for dev in partners:
        pl.semaphore_signal(barrier, inc=1, device_id=dev, device_id_type=MESH)

    def cols(ch):
        return pl.ds(pl.multiple_of(ch * kc, kc), kc)

    def own_copy(ch):
        return pltpu.make_async_copy(
            tok.at[:, cols(ch)], x.at[ch, core, yy, zz], s_tok.at[ch]
        )

    def z_copy(ch, d):
        return remote(
            tok.at[:, cols(ch)], x.at[ch, core, yy, zz],
            zs.at[ch, d - 1], zr.at[ch, d - 1], at(far(d), yy, core),
        )

    def z_wait(ch, d):
        remote(
            tok.at[:, cols(ch)], x.at[ch, core, yy, near(d)],
            zs.at[ch, d - 1], zr.at[ch, d - 1], at(far(d), yy, core),
        ).wait_recv()

    def y_copy(ch, side):
        part = x.at[ch, core, side]
        return remote(part, part, ys.at[ch], yr.at[ch], at(zz, 1 - yy, core))

    def c_copy(ch, side):
        part = x.at[ch, side]
        return remote(part, part, cs.at[ch], cr.at[ch], at(zz, yy, 1 - core))

    own_p = pltpu.make_async_copy(ss.at[:, :, :, core], pbuf.at[pl.ds(0, keep)], s_p.at[0])
    far_p = remote(
        ss.at[:, :, :, 1 - core], pbuf.at[pl.ds(keep, keep)], ps.at[0], pr.at[0],
        at(zz, yy, 1 - core),
    )

    def ry_copy(z):
        return remote(
            sbuf.at[z], qbuf.at[yy, z], rys.at[z], ryr.at[z], at(zz, 1 - yy, core)
        )

    def rz_copy(d):
        return remote(
            tbuf.at[far(d)], fbuf.at[zz], rzs.at[d - 1], rzr.at[d - 1], at(far(d), yy, core)
        )

    def l_copy(hop, src, dst, dev):
        return remote(src, dst, ls.at[hop], lr.at[hop], dev)

    l_core = l_copy(0, lc.at[core], lc.at[core], at(zz, yy, 1 - core))
    l_y = l_copy(1, ly.at[yy], ly.at[yy], at(zz, 1 - yy, core))

    def l_z(d):
        return l_copy(1 + d, lz.at[zz], lz.at[zz], at(far(d), yy, core))

    def own_loop(ch, _):
        own_copy(ch).start()
        return 0

    lax.fori_loop(0, CHUNKS, own_loop, 0)
    for j in range(SLOTS // 2):
        w_copy(wg, j, 0).start()
        w_copy(wu, j, 1).start()
    own_p.start()
    slot = omap[ids[0]]
    kslot = lax.rem(slot, keep)
    owner = slot // keep
    oc = lax.rem(owner, 2)
    oy = lax.rem(owner // 2, 2)
    oz = owner // 4
    pick = jnp.where(oc == core, 0, keep) + kslot
    ag[...] = jnp.zeros_like(ag)
    au[...] = jnp.zeros_like(au)
    lacc[...] = jnp.zeros_like(lacc)
    pl.semaphore_wait(barrier, len(partners))

    def z_loop(ch, _):
        for d in range(1, nz):
            z_copy(ch, d).start()
        return 0

    lax.fori_loop(0, CHUNKS, z_loop, 0)
    far_p.start()

    def step(i, _):
        @pl.when(i < CHUNKS)
        def _():
            own_copy(i).wait()
            for d in range(1, nz):
                z_wait(i, d)
            y_copy(i, yy).start()

        @pl.when((i >= 1) & (i < CHUNKS + 1))
        def _():
            ch = i - 1
            y_copy(ch, 1 - yy).wait_recv()
            c_copy(ch, core).start()

        @pl.when((i >= 2) & (i < CHUNKS + 2))
        def _():
            ch = i - 2
            c_copy(ch, 1 - core).wait_recv()
            for z in range(nz):
                for y in range(2):
                    a = x[ch, 0, y, z].astype(jnp.float32)
                    b = x[ch, 1, y, z].astype(jnp.float32)
                    m = 16 * (z * 2 + y)
                    xf[ch, m:m + 16, :] = jnp.concatenate([a, b], 0).astype(jnp.bfloat16)
            size = f1.shape[3]
            for s in range(sub):
                lacc[...] += lax.dot_general(
                    f1[kslot, ch * sub + s], xf[ch, :, s * size:(s + 1) * size],
                    (((1,), (1,)), ((), ())), preferred_element_type=jnp.float32,
                )

        @pl.when(i == R1_AT)
        def _():
            own_p.wait()
            far_p.wait_recv()
            for d in (*range(1, nz), 0):
                z = far(d)
                sbuf[z] = pbuf[pick, z, 1 - yy]
                ry_copy(z).start()
                qbuf[yy, z] = pbuf[pick, z, yy]

        for d in (*range(1, nz), 0):
            @pl.when(i == R2_AT[d])
            def _():
                z = far(d)
                remote(
                    sbuf.at[z], qbuf.at[1 - yy, z], rys.at[z], ryr.at[z],
                    at(zz, 1 - yy, core),
                ).wait_recv()
                tbuf[z] = jnp.where(oy == yy, qbuf[yy, z], qbuf[1 - yy, z])
                if d:
                    rz_copy(d).start()
                else:
                    fbuf[zz] = tbuf[zz]

        @pl.when(i == CHUNKS + 1)
        def _():
            lc[core] = lacc[...].astype(jnp.bfloat16)
            l_core.start()

        @pl.when(i == CHUNKS + 2)
        def _():
            l_copy(0, lc.at[core], lc.at[1 - core], at(zz, yy, 1 - core)).wait_recv()
            ly[yy] = lc[oc]
            l_y.start()

        @pl.when(i >= 3)
        def _():
            ch = i - 3
            for half, src, acc in ((0, wg, ag), (1, wu, au)):
                w_copy(src, ch, half).wait()
                slot_w = lax.rem(ch * 2 + half, SLOTS)
                for n in range(0, width, 256):
                    acc[:, n:n + 256] += jnp.dot(
                        xf[ch], w[slot_w, :, n:n + 256], preferred_element_type=jnp.float32
                    )

                @pl.when(ch + SLOTS // 2 < CHUNKS)
                def _():
                    w_copy(src, ch + SLOTS // 2, half).start()

        return 0

    lax.fori_loop(0, CHUNKS + 3, step, 0)

    l_copy(1, ly.at[yy], ly.at[1 - yy], at(zz, 1 - yy, core)).wait_recv()
    lz[zz] = ly[oy]
    for d in range(1, nz):
        l_z(d).start()
    for d in range(1, nz):
        remote(
            tbuf.at[far(d)], fbuf.at[near(d)], rzs.at[d - 1], rzr.at[d - 1],
            at(far(d), yy, core),
        ).wait_recv()
    for d in range(1, nz):
        l_copy(1 + d, lz.at[zz], lz.at[near(d)], at(far(d), yy, core)).wait_recv()
    lstage[...] = lz[oz]
    rank = lstage.shape[0] // 2
    dims = (((0,), (0,)), ((), ()))
    for n in range(0, width, 256):
        g = ag[:, n:n + 256] + lax.dot_general(
            lstage[:rank], fbuf[oz, :rank, n:n + 256], dims, preferred_element_type=jnp.float32
        )
        u = au[:, n:n + 256] + lax.dot_general(
            lstage[rank:], fbuf[oz, rank:, n:n + 256], dims, preferred_element_type=jnp.float32
        )
        out[:, n:n + 256] = (g / (1.0 + jnp.exp(-g)) * u).astype(out.dtype)

    def drain(ch, _):
        for d in range(1, nz):
            z_copy(ch, d).wait_send()
        y_copy(ch, yy).wait_send()
        c_copy(ch, core).wait_send()
        return 0

    lax.fori_loop(0, CHUNKS, drain, 0)
    far_p.wait_send()
    for z in range(nz):
        ry_copy(z).wait_send()
    for d in range(1, nz):
        rz_copy(d).wait_send()
        l_z(d).wait_send()
    l_core.wait_send()
    l_y.wait_send()


def fused(tensor, tokens, gate_weight, up_weight, first_store, second_store, adapter_ids, owner_map):
    nz = tensor // 4
    keep = first_store.shape[0]
    doubled, width = second_store.shape[2:]
    depth = tokens.shape[1]
    kc = depth // CHUNKS
    rows = tokens.shape[0] * tensor
    second = second_store.reshape(keep, nz, 2, 2, doubled, width)
    any_, vmem, smem = (
        pl.BlockSpec(memory_space=s) for s in (pl.ANY, pltpu.VMEM, pltpu.SMEM)
    )
    bf, f32 = jnp.bfloat16, jnp.float32
    dma = pltpu.SemaphoreType.DMA
    return pl.pallas_call(
        functools.partial(kernel, nz, keep),
        out_shape=jax.ShapeDtypeStruct((rows, width), bf),
        in_specs=[any_, any_, any_, vmem, any_, smem, smem],
        out_specs=vmem,
        scratch_shapes=[
            pltpu.VMEM((CHUNKS, 2, 2, nz, tokens.shape[0], kc), bf),
            pltpu.VMEM((CHUNKS, rows, kc), bf),
            pltpu.VMEM((SLOTS, kc, width), bf),
            pltpu.VMEM((rows, width), f32),
            pltpu.VMEM((rows, width), f32),
            pltpu.VMEM((2 * keep, nz, 2, doubled, width), bf),
            pltpu.VMEM((nz, doubled, width), bf),
            pltpu.VMEM((2, nz, doubled, width), bf),
            pltpu.VMEM((nz, doubled, width), bf),
            pltpu.VMEM((nz, doubled, width), bf),
            pltpu.VMEM((doubled, rows), f32),
            pltpu.VMEM((doubled, rows), bf),
            pltpu.VMEM((2, doubled, rows), bf),
            pltpu.VMEM((2, doubled, rows), bf),
            pltpu.VMEM((nz, doubled, rows), bf),
            dma((CHUNKS,)), dma((SLOTS,)), dma((1,)),
            dma((CHUNKS, nz - 1)), dma((CHUNKS, nz - 1)),
            dma((CHUNKS,)), dma((CHUNKS,)), dma((CHUNKS,)), dma((CHUNKS,)),
            dma((1,)), dma((1,)), dma((nz,)), dma((nz,)), dma((nz - 1,)), dma((nz - 1,)),
            dma((nz + 1,)), dma((nz + 1,)),
        ],
        compiler_params=pltpu.CompilerParams(
            collective_id=0, has_side_effects=True, vmem_limit_bytes=63 * 1024 * 1024
        ),
        cost_estimate=pl.CostEstimate(
            flops=4 * rows * depth * width, bytes_accessed=4 * depth * width,
            transcendentals=rows * width,
        ),
    )(tokens, gate_weight, up_weight, first_store, second, adapter_ids, owner_map)


def solution(mesh):
    tensor = mesh.shape["tensor"]

    def per_device(*args):
        if tensor == 16 and args[5].shape[0] == 1:
            return fused(tensor, *args)
        return general(*args)

    placed = (
        P(("groups", "tensor"), None),
        P(None, "tensor"),
        P(None, "tensor"),
        P(("groups", "tensor"), None, None, None),
        P(("groups", "tensor"), None, None, None),
        P("groups"),
        P("groups"),
    )
    return jax.shard_map(
        per_device, mesh=mesh, in_specs=placed, out_specs=P("groups", "tensor"), check_vma=False
    )
```

```python
import functools
import jax
import jax.numpy as jnp
from jax import lax
from jax.experimental import pallas as pl
from jax.experimental.pallas import tpu as pltpu
from jax.sharding import PartitionSpec as P

PLEN = 128
CHUNKS = 4
SLOTS = 6
R1_AT, R2_AT = 3, (6, 5, 6, 6)
MESH = pl.DeviceIdType.MESH


def spread(value, axis, root):
    mine = lax.axis_index(axis) == root
    return lax.psum(jnp.where(mine, value, jnp.zeros_like(value)), axis)


def general(tokens, gate_weight, up_weight, first_store, second_store, adapter_ids, owner_map):
    own_index = lax.axis_index("tensor")
    tok_dev = tokens.shape[0]
    prompts = adapter_ids.shape[0]
    keep_count = first_store.shape[0]
    doubled = second_store.shape[2]
    rank = doubled // 2
    width = gate_weight.shape[1]
    matches = adapter_ids[:, None] == jnp.arange(owner_map.shape[0], dtype=jnp.int32)[None, :]
    slots = jnp.sum(jnp.where(matches, owner_map[None, :], 0), axis=1)
    own_prompt = own_index * tok_dev // PLEN

    def fetch_step(prompt, held):
        slot = lax.dynamic_index_in_dim(slots, prompt, 0, keepdims=False)
        piece = lax.dynamic_index_in_dim(first_store, slot % keep_count, 0, keepdims=False)
        landed = spread(piece, "tensor", slot // keep_count)
        return jnp.where(prompt == own_prompt, landed, held)

    blocked = lax.fori_loop(0, prompts, fetch_step, jnp.zeros(first_store.shape[1:], jnp.bfloat16))
    factor = jnp.transpose(blocked, (1, 0, 2)).reshape(doubled, tokens.shape[1])
    lowrank = jnp.dot(tokens, factor.T, preferred_element_type=jnp.float32).astype(jnp.bfloat16)
    whole, low_all = (
        lax.all_gather(tokens, "tensor", axis=0, tiled=True),
        lax.all_gather(lowrank, "tensor", axis=0, tiled=True),
    )
    spread_second = lax.all_to_all(second_store, "tensor", split_axis=1, concat_axis=0, tiled=True)
    spread_second = spread_second.reshape(spread_second.shape[0], 2, rank, width)
    picked_second = jnp.take(spread_second, slots, axis=0)
    low_four = low_all.reshape(prompts, PLEN, 2, rank)
    delta = jnp.einsum(
        "ptgr,pgrf->gptf", low_four, picked_second, preferred_element_type=jnp.float32
    )
    delta = delta.reshape(2, prompts * PLEN, width)
    gate = jnp.dot(whole, gate_weight, preferred_element_type=jnp.float32) + delta[0]
    lifted = jnp.dot(whole, up_weight, preferred_element_type=jnp.float32) + delta[1]
    return (jax.nn.silu(gate) * lifted).astype(jnp.bfloat16)


def kernel(
    nz, keep,
    tok, wg, wu, f1, ss, ids, omap, out,
    x, xf, w, ag, au, pbuf, sbuf, qbuf, tbuf, fbuf, lacc, lstage, lc, ly, lz,
    s_tok, s_w, s_p, zs, zr, ys, yr, cs, cr, ps, pr, rys, ryr, rzs, rzr, ls, lr,
):
    me = lax.axis_index("tensor")
    core = lax.rem(me, 2)
    yy = lax.rem(me // 2, 2)
    zz = me // 4
    kc = xf.shape[2]
    width = wg.shape[1]
    sub = kc // f1.shape[3]
    nw = 2 * CHUNKS

    def at(z, y, c):
        return {"tensor": z * 4 + y * 2 + c}

    def far(d):
        return lax.rem(zz + d, nz)

    def near(d):
        return lax.rem(zz + nz - d, nz)

    def remote(src, dst, send, recv, dev):
        return pltpu.make_async_remote_copy(
            src_ref=src, dst_ref=dst, send_sem=send, recv_sem=recv,
            device_id=dev, device_id_type=MESH,
        )

    def w_copy(src, chunk, half):
        slot = lax.rem(chunk * 2 + half, SLOTS)
        rows = pl.ds(pl.multiple_of(chunk * kc, kc), kc)
        return pltpu.make_async_copy(src.at[rows, :], w.at[slot], s_w.at[slot])

    partners = [at(zz, yy, 1 - core), at(zz, 1 - yy, core)]
    partners += [at(far(d), yy, core) for d in range(1, nz)]
    barrier = pltpu.get_barrier_semaphore()
    for dev in partners:
        pl.semaphore_signal(barrier, inc=1, device_id=dev, device_id_type=MESH)

    def cols(ch):
        return pl.ds(pl.multiple_of(ch * kc, kc), kc)

    def own_copy(ch):
        return pltpu.make_async_copy(
            tok.at[:, cols(ch)], x.at[ch, core, yy, zz], s_tok.at[ch]
        )

    def z_copy(ch, d):
        return remote(
            tok.at[:, cols(ch)], x.at[ch, core, yy, zz],
            zs.at[ch, d - 1], zr.at[ch, d - 1], at(far(d), yy, core),
        )

    def z_wait(ch, d):
        remote(
            tok.at[:, cols(ch)], x.at[ch, core, yy, near(d)],
            zs.at[ch, d - 1], zr.at[ch, d - 1], at(far(d), yy, core),
        ).wait_recv()

    def y_copy(ch, side):
        part = x.at[ch, core, side]
        return remote(part, part, ys.at[ch], yr.at[ch], at(zz, 1 - yy, core))

    def c_copy(ch, side):
        part = x.at[ch, side]
        return remote(part, part, cs.at[ch], cr.at[ch], at(zz, yy, 1 - core))

    own_p = pltpu.make_async_copy(ss.at[:, :, :, core], pbuf.at[pl.ds(0, keep)], s_p.at[0])
    far_p = remote(
        ss.at[:, :, :, 1 - core], pbuf.at[pl.ds(keep, keep)], ps.at[0], pr.at[0],
        at(zz, yy, 1 - core),
    )

    def ry_copy(z):
        return remote(
            sbuf.at[z], qbuf.at[yy, z], rys.at[z], ryr.at[z], at(zz, 1 - yy, core)
        )

    def rz_copy(d):
        return remote(
            tbuf.at[far(d)], fbuf.at[zz], rzs.at[d - 1], rzr.at[d - 1], at(far(d), yy, core)
        )

    def l_copy(hop, src, dst, dev):
        return remote(src, dst, ls.at[hop], lr.at[hop], dev)

    l_core = l_copy(0, lc.at[core], lc.at[core], at(zz, yy, 1 - core))
    l_y = l_copy(1, ly.at[yy], ly.at[yy], at(zz, 1 - yy, core))

    def l_z(d):
        return l_copy(1 + d, lz.at[zz], lz.at[zz], at(far(d), yy, core))

    def own_loop(ch, _):
        own_copy(ch).start()
        return 0

    lax.fori_loop(0, CHUNKS, own_loop, 0)
    for j in range(SLOTS // 2):
        w_copy(wg, j, 0).start()
        w_copy(wu, j, 1).start()
    own_p.start()
    slot = omap[ids[0]]
    kslot = lax.rem(slot, keep)
    owner = slot // keep
    oc = lax.rem(owner, 2)
    oy = lax.rem(owner // 2, 2)
    oz = owner // 4
    pick = jnp.where(oc == core, 0, keep) + kslot
    ag[...] = jnp.zeros_like(ag)
    au[...] = jnp.zeros_like(au)
    lacc[...] = jnp.zeros_like(lacc)
    pl.semaphore_wait(barrier, len(partners))

    def z_loop(ch, _):
        for d in range(1, nz):
            z_copy(ch, d).start()
        return 0

    lax.fori_loop(0, CHUNKS, z_loop, 0)
    far_p.start()

    def step(i, _):
        @pl.when(i < CHUNKS)
        def _():
            own_copy(i).wait()
            for d in range(1, nz):
                z_wait(i, d)
            y_copy(i, yy).start()

        @pl.when((i >= 1) & (i < CHUNKS + 1))
        def _():
            ch = i - 1
            y_copy(ch, 1 - yy).wait_recv()
            c_copy(ch, core).start()

        @pl.when((i >= 2) & (i < CHUNKS + 2))
        def _():
            ch = i - 2
            c_copy(ch, 1 - core).wait_recv()
            for z in range(nz):
                for y in range(2):
                    a = x[ch, 0, y, z].astype(jnp.float32)
                    b = x[ch, 1, y, z].astype(jnp.float32)
                    m = 16 * (z * 2 + y)
                    xf[ch, m:m + 16, :] = jnp.concatenate([a, b], 0).astype(jnp.bfloat16)
            size = f1.shape[3]
            for s in range(sub):
                lacc[...] += lax.dot_general(
                    f1[kslot, ch * sub + s], xf[ch, :, s * size:(s + 1) * size],
                    (((1,), (1,)), ((), ())), preferred_element_type=jnp.float32,
                )

        @pl.when(i == R1_AT)
        def _():
            own_p.wait()
            far_p.wait_recv()
            for d in (*range(1, nz), 0):
                z = far(d)
                sbuf[z] = pbuf[pick, z, 1 - yy]
                ry_copy(z).start()
                qbuf[yy, z] = pbuf[pick, z, yy]

        for d in (*range(1, nz), 0):
            @pl.when(i == R2_AT[d])
            def _():
                z = far(d)
                remote(
                    sbuf.at[z], qbuf.at[1 - yy, z], rys.at[z], ryr.at[z],
                    at(zz, 1 - yy, core),
                ).wait_recv()
                tbuf[z] = jnp.where(oy == yy, qbuf[yy, z], qbuf[1 - yy, z])
                if d:
                    rz_copy(d).start()
                else:
                    fbuf[zz] = tbuf[zz]

        @pl.when(i == CHUNKS + 1)
        def _():
            lc[core] = lacc[...].astype(jnp.bfloat16)
            l_core.start()

        @pl.when(i == CHUNKS + 2)
        def _():
            l_copy(0, lc.at[core], lc.at[1 - core], at(zz, yy, 1 - core)).wait_recv()
            ly[yy] = lc[oc]
            l_y.start()

        @pl.when(i >= 3)
        def _():
            ch = i - 3
            for half, src, acc in ((0, wg, ag), (1, wu, au)):
                w_copy(src, ch, half).wait()
                slot_w = lax.rem(ch * 2 + half, SLOTS)
                for n in range(0, width, 256):
                    acc[:, n:n + 256] += jnp.dot(
                        xf[ch], w[slot_w, :, n:n + 256], preferred_element_type=jnp.float32
                    )

                @pl.when(ch + SLOTS // 2 < CHUNKS)
                def _():
                    w_copy(src, ch + SLOTS // 2, half).start()

        return 0

    lax.fori_loop(0, CHUNKS + 3, step, 0)

    l_copy(1, ly.at[yy], ly.at[1 - yy], at(zz, 1 - yy, core)).wait_recv()
    lz[zz] = ly[oy]
    for d in range(1, nz):
        l_z(d).start()
    for d in range(1, nz):
        remote(
            tbuf.at[far(d)], fbuf.at[near(d)], rzs.at[d - 1], rzr.at[d - 1],
            at(far(d), yy, core),
        ).wait_recv()
    for d in range(1, nz):
        l_copy(1 + d, lz.at[zz], lz.at[near(d)], at(far(d), yy, core)).wait_recv()
    lstage[...] = lz[oz]
    rank = lstage.shape[0] // 2
    dims = (((0,), (0,)), ((), ()))
    for n in range(0, width, 256):
        g = ag[:, n:n + 256] + lax.dot_general(
            lstage[:rank], fbuf[oz, :rank, n:n + 256], dims, preferred_element_type=jnp.float32
        )
        u = au[:, n:n + 256] + lax.dot_general(
            lstage[rank:], fbuf[oz, rank:, n:n + 256], dims, preferred_element_type=jnp.float32
        )
        out[:, n:n + 256] = (g / (1.0 + jnp.exp(-g)) * u).astype(out.dtype)

    def drain(ch, _):
        for d in range(1, nz):
            z_copy(ch, d).wait_send()
        y_copy(ch, yy).wait_send()
        c_copy(ch, core).wait_send()
        return 0

    lax.fori_loop(0, CHUNKS, drain, 0)
    far_p.wait_send()
    for z in range(nz):
        ry_copy(z).wait_send()
    for d in range(1, nz):
        rz_copy(d).wait_send()
        l_z(d).wait_send()
    l_core.wait_send()
    l_y.wait_send()


def fused(tensor, tokens, gate_weight, up_weight, first_store, second_store, adapter_ids, owner_map):
    nz = tensor // 4
    keep = first_store.shape[0]
    doubled, width = second_store.shape[2:]
    depth = tokens.shape[1]
    kc = depth // CHUNKS
    rows = tokens.shape[0] * tensor
    second = second_store.reshape(keep, nz, 2, 2, doubled, width)
    any_, vmem, smem = (
        pl.BlockSpec(memory_space=s) for s in (pl.ANY, pltpu.VMEM, pltpu.SMEM)
    )
    bf, f32 = jnp.bfloat16, jnp.float32
    dma = pltpu.SemaphoreType.DMA
    return pl.pallas_call(
        functools.partial(kernel, nz, keep),
        out_shape=jax.ShapeDtypeStruct((rows, width), bf),
        in_specs=[any_, any_, any_, vmem, any_, smem, smem],
        out_specs=vmem,
        scratch_shapes=[
            pltpu.VMEM((CHUNKS, 2, 2, nz, tokens.shape[0], kc), bf),
            pltpu.VMEM((CHUNKS, rows, kc), bf),
            pltpu.VMEM((SLOTS, kc, width), bf),
            pltpu.VMEM((rows, width), f32),
            pltpu.VMEM((rows, width), f32),
            pltpu.VMEM((2 * keep, nz, 2, doubled, width), bf),
            pltpu.VMEM((nz, doubled, width), bf),
            pltpu.VMEM((2, nz, doubled, width), bf),
            pltpu.VMEM((nz, doubled, width), bf),
            pltpu.VMEM((nz, doubled, width), bf),
            pltpu.VMEM((doubled, rows), f32),
            pltpu.VMEM((doubled, rows), bf),
            pltpu.VMEM((2, doubled, rows), bf),
            pltpu.VMEM((2, doubled, rows), bf),
            pltpu.VMEM((nz, doubled, rows), bf),
            dma((CHUNKS,)), dma((SLOTS,)), dma((1,)),
            dma((CHUNKS, nz - 1)), dma((CHUNKS, nz - 1)),
            dma((CHUNKS,)), dma((CHUNKS,)), dma((CHUNKS,)), dma((CHUNKS,)),
            dma((1,)), dma((1,)), dma((nz,)), dma((nz,)), dma((nz - 1,)), dma((nz - 1,)),
            dma((nz + 1,)), dma((nz + 1,)),
        ],
        compiler_params=pltpu.CompilerParams(
            collective_id=0, has_side_effects=True, vmem_limit_bytes=63 * 1024 * 1024
        ),
        cost_estimate=pl.CostEstimate(
            flops=4 * rows * depth * width, bytes_accessed=4 * depth * width,
            transcendentals=rows * width,
        ),
    )(tokens, gate_weight, up_weight, first_store, second, adapter_ids, owner_map)


def solution(mesh):
    tensor = mesh.shape["tensor"]

    def per_device(*args):
        if tensor == 16 and args[5].shape[0] == 1:
            return fused(tensor, *args)
        return general(*args)

    placed = (
        P(("groups", "tensor"), None),
        P(None, "tensor"),
        P(None, "tensor"),
        P(("groups", "tensor"), None, None, None),
        P(("groups", "tensor"), None, None, None),
        P("groups"),
        P("groups"),
    )
    return jax.shard_map(
        per_device, mesh=mesh, in_specs=placed, out_specs=P("groups", "tensor"), check_vma=False
    )
```
